256 devices in a mesh: grid: 4 (over x), slab: 64 (over y, z, core).
Axes of the slice: x: 4, y: 4, z: 8, core: 2. Of those that a mesh axis runs over, the one named last changes fastest.
Arguments:
- state: float32 [4, 5, 256, 256, 128], P('grid', None, 'slab'), may hold values from -2 to 5, as said below
- jacobian: float32 [4, 256, 256, 128], P('grid', 'slab'), may hold values from 0.5 to 2
- iblank: int32 [4, 256, 256, 1], P('grid', 'slab'), may hold values from 0 to 2
- donor_blocks: int32 [4, 4096, 2], P('grid', 'slab'), may hold values from 0 to 1023
- recv_blocks: int32 [4, 4096, 2], P('grid', 'slab'), may hold values from 0 to 1023, as said below
- deriv_a: float32 [4, 256, 256], P('grid')
- deriv_b: float32 [4, 256, 256], P('grid')
- filter_a: float32 [4, 256, 256], P('grid')
- filter_b: float32 [4, 256, 256], P('grid')
Outputs:
- advanced: float32 [4, 5, 256, 256, 128], P('grid', None, 'slab')
The draws below stay inside these ranges and needn't reach their ends.
Inputs may be any that keep to these rules, and one draw needn't show every extreme that they name: `state`: state variable 0 (density) lies in 0.5 to 2, variable 4 (energy) in 2 to 5, momenta in -2 to 2. `recv_blocks`: within the rows of one slab position the entries are distinct; no block flagged 0 is among them, and every block flagged 2 is.
All inputs are finite; a program needn't handle non-finite values.
Results may differ from the reference program's by a relative error of at most 0.0003.
Values sent between devices are 32-bit elements; how exact they have to be, the bound alone decides.
No kernel may reach another device: no remote copies, remote signals or barrier semaphores. Data moves between devices by JAX's collectives and lax.ppermute only.
A program may use at most 64 MiB of HBM per device.

```python
import math
import jax
import jax.numpy as jnp
from jax import lax

V = 5
NA = 256
NB = 256
NC = 128
BLOCK = 128
CAP = 2
NGRIDS = 4
BLOCKS_DEV = 1024
N_SLAB = 64


def layout_perm(key):
    keys = jax.random.split(key, NGRIDS * N_SLAB)
    return jax.vmap(lambda single: jax.random.permutation(single, BLOCKS_DEV))(keys).astype(jnp.int32)


def banded(noise, width, scale, diagonal):
    size = noise.shape[-1]
    rows = jnp.arange(size)[:, None]
    cols = jnp.arange(size)[None, :]
    envelope = jnp.exp(-jnp.abs(rows - cols).astype(jnp.float32) / width)
    return scale * envelope * noise + diagonal * (rows == cols).astype(jnp.float32)


def draw_recv_blocks(key, part):
    perms = layout_perm(key)
    chosen = perms[:, :N_SLAB * CAP]
    return chosen.reshape(NGRIDS, N_SLAB * N_SLAB, CAP).astype(jnp.int32)


def draw_iblank(key, part):
    perms = layout_perm(key)
    key = jax.random.fold_in(key, 5)
    first_key, second_key = jax.random.split(key)
    positions = jnp.arange(BLOCKS_DEV)[None, :]
    live = jax.random.randint(first_key, (NGRIDS * N_SLAB, BLOCKS_DEV), 0, 4) > 0
    holes = jax.random.randint(second_key, (NGRIDS * N_SLAB, BLOCKS_DEV), 0, 6) == 0
    values = jnp.where(positions < N_SLAB * CAP, jnp.where(live, 2, 1), jnp.where(holes, 0, 1)).astype(jnp.int32)
    flags = jax.vmap(lambda order, vals: jnp.zeros((BLOCKS_DEV,), jnp.int32).at[order].set(vals))(perms, values)
    return flags.reshape(NGRIDS, NA, NB, NC // BLOCK)


def draw_state(key, part):
    key = jax.random.fold_in(key, 19)
    keys = jax.random.split(key, 3)
    shape = (NGRIDS, 1, NA, NB, NC)
    density = jnp.exp(jax.random.uniform(keys[0], shape, jnp.float32, math.log(0.5), math.log(2.0)))
    momentum = jnp.clip(0.5 * jax.random.normal(keys[1], (NGRIDS, 3, NA, NB, NC), jnp.float32), -2.0, 2.0)
    energy = jax.random.uniform(keys[2], shape, jnp.float32, 2.0, 4.0)
    return jnp.concatenate([density, momentum, energy], 1)


def draw_deriv_a(key, part):
    key = jax.random.fold_in(key, 11)
    shape = (NGRIDS, NA, NA)
    noise = jax.random.normal(key, shape, jnp.float32)
    return banded(noise, 4.0 * NA / N_SLAB, 0.18, 0.0)


def draw_deriv_b(key, part):
    key = jax.random.fold_in(key, 13)
    shape = (NGRIDS, NB, NB)
    noise = jax.random.normal(key, shape, jnp.float32)
    return banded(noise, NB / 16.0, 0.18, 0.0)


def draw_filter_a(key, part):
    key = jax.random.fold_in(key, 17)
    shape = (NGRIDS, NA, NA)
    noise = jax.random.normal(key, shape, jnp.float32)
    return banded(noise, 4.0 * NA / N_SLAB, 0.05, 0.8)


def draw_filter_b(key, part):
    key = jax.random.fold_in(key, 23)
    shape = (NGRIDS, NB, NB)
    noise = jax.random.normal(key, shape, jnp.float32)
    return banded(noise, NB / 16.0, 0.05, 0.8)


def place_ends(array, stream_key, low, top_value):
    place = [jax.random.randint(jax.random.fold_in(stream_key, axis), (), 0, length) for axis, length in enumerate(array.shape)]
    main_axis = array.shape.index(max(array.shape))
    next_to = place[:main_axis] + [(place[main_axis] + 1) % array.shape[main_axis]] + place[main_axis + 1:]
    return array.at[tuple(place)].set(low).at[tuple(next_to)].set(top_value)


def block_scale(stream_key, dims, shards, low, top_value):
    factor_of, own = 1.0, jax.random.fold_in(stream_key, 6)
    for dim, blocks in shards:
        heights = jnp.exp(jax.random.uniform(jax.random.fold_in(own, dim), (blocks,), jnp.float32, low / len(shards), top_value / len(shards)))
        factor_of = factor_of * jnp.repeat(heights, dims[dim] // blocks).reshape([-1 if axis == dim else 1 for axis in range(len(dims))])
    return factor_of


def setup_inputs(seed: int = 0) -> dict:
    key_of = jax.random.split(jax.random.key(seed), 10)
    state = draw_state(jax.random.fold_in(key_of[9], 71), 0)
    jacobian = jnp.clip(jnp.exp(math.log(2.0) - 1.3862944 * jax.random.uniform(key_of[1], (NGRIDS, NA, NB, NC), jnp.float32) ** block_scale(key_of[1], (NGRIDS, NA, NB, NC), ((0, 4), (1, 64)), -0.2, 0.2)), 0.5, 2.0)
    iblank = draw_iblank(jax.random.fold_in(key_of[9], 71), 0)
    donor_blocks = place_ends(jax.random.randint(key_of[3], (NGRIDS, N_SLAB * N_SLAB, CAP), 0, BLOCKS_DEV), jax.random.fold_in(key_of[3], 1), 0, BLOCKS_DEV - 1).astype(jnp.int32)
    recv_blocks = draw_recv_blocks(jax.random.fold_in(key_of[9], 71), 0)
    deriv_a = draw_deriv_a(jax.random.fold_in(key_of[9], 71), 0)
    deriv_b = draw_deriv_b(jax.random.fold_in(key_of[9], 71), 0)
    filter_a = draw_filter_a(jax.random.fold_in(key_of[9], 71), 0)
    filter_b = draw_filter_b(jax.random.fold_in(key_of[9], 71), 0)
    return dict(state=state, jacobian=jacobian, iblank=iblank, donor_blocks=donor_blocks, recv_blocks=recv_blocks, deriv_a=deriv_a, deriv_b=deriv_b, filter_a=filter_a, filter_b=filter_b)


section_weight = 0.3


def fluxes(prepared):
    density = prepared[0]
    momentum_a = prepared[1]
    momentum_b = prepared[2]
    momentum_c = prepared[3]
    energy = prepared[4]
    inverse = 1.0 / density
    pressure = 0.4 * (energy - 0.5 * (momentum_a * momentum_a + momentum_b * momentum_b + momentum_c * momentum_c) * inverse)
    flux_a = jnp.stack([momentum_a, momentum_a * momentum_a * inverse + pressure, momentum_a * momentum_b * inverse,
                        momentum_a * momentum_c * inverse, (energy + pressure) * momentum_a * inverse])
    flux_b = jnp.stack([momentum_b, momentum_a * momentum_b * inverse, momentum_b * momentum_b * inverse + pressure,
                        momentum_b * momentum_c * inverse, (energy + pressure) * momentum_b * inverse])
    return flux_a, flux_b


def along_first(matrix, field):
    return jnp.einsum('ij,vjbc->vibc', matrix, field, precision=lax.Precision.HIGHEST)


def along_second(matrix, field):
    return jnp.einsum('ij,vajc->vaic', matrix, field, precision=lax.Precision.HIGHEST)


def reference(state, jacobian, iblank, donor_blocks, recv_blocks, deriv_a, deriv_b, filter_a, filter_b):
    def one_grid(grid_index):
        partner = jnp.bitwise_xor(grid_index, 1)
        own_flat = jnp.concatenate([state[grid_index], jacobian[grid_index][None]], 0).reshape(V + 1, N_SLAB * BLOCKS_DEV, BLOCK)
        other_flat = jnp.concatenate([state[partner], jacobian[partner][None]], 0).reshape(V + 1, N_SLAB * BLOCKS_DEV, BLOCK)
        offsets = (jnp.arange(N_SLAB, dtype=jnp.int32) * BLOCKS_DEV)[:, None, None]
        donors = donor_blocks[partner].reshape(N_SLAB, N_SLAB, CAP) + offsets
        donors = jnp.transpose(donors, (1, 0, 2)).reshape(-1)
        donated = other_flat[:, donors, :]
        targets = (recv_blocks[grid_index].reshape(N_SLAB, N_SLAB, CAP) + offsets).reshape(-1)
        present = own_flat[:, targets, :]
        weight_donor = donated[V]
        weight_own = present[V]
        blended = (weight_donor * donated[:V] + weight_own * present[:V]) / (weight_donor + weight_own)
        flags = iblank[grid_index].reshape(-1)
        live = (flags[targets] == 2)[None, :, None]
        prepared = own_flat[:V].at[:, targets, :].set(jnp.where(live, blended, present[:V]))
        freestream = jnp.asarray([1.0, 0.5, 0.0, 0.0, 2.5], prepared.dtype)
        holes = (flags == 0)[None, :, None]
        prepared = jnp.where(holes, freestream[:, None, None], prepared).reshape(V, NA, NB, NC)
        flux_a, flux_b = fluxes(prepared)
        sectioned = prepared - section_weight * (along_first(deriv_a[grid_index], flux_a) + along_second(deriv_b[grid_index], flux_b))
        return along_first(filter_a[grid_index], along_second(filter_b[grid_index], sectioned))

    return lax.map(one_grid, jnp.arange(NGRIDS, dtype=jnp.int32))
```

```python
import jax
import jax.numpy as jnp
from jax import lax
from jax.experimental import pallas as pl
from jax.experimental.pallas import tpu as pltpu
from jax.sharding import PartitionSpec as P

V = 5
R = 4
N = 64
B = 256
L = 128
H = 24
C = 2 * H
Q = 2 * V * R
SLOTS = 128
EXTRA = (20, 21, 22, 23, 44, 45, 46, 47)
FREE = (1.0, 0.5, 0.0, 0.0, 2.5)

section_weight = 0.3
f32, bf16, i32 = jnp.float32, jnp.bfloat16, jnp.int32
VMEM = pl.BlockSpec(memory_space=pltpu.VMEM)
SMEM = pl.BlockSpec(memory_space=pltpu.SMEM)
ANY = pl.BlockSpec(memory_space=pl.ANY)


def params(mib):
    return pltpu.CompilerParams(vmem_limit_bytes=mib * 2**20)


def cost(nbytes, flops=0):
    return pl.CostEstimate(flops=flops, bytes_accessed=nbytes, transcendentals=0)


def gather_kernel(slots, state, jacobian, out):
    def body(k, carry):
        t = slots[k]
        out[pl.ds(k, V, stride=SLOTS), :] = state[pl.ds(t, V, stride=R * B), :]
        out[pl.ds(V * SLOTS + k, 1), :] = jacobian[pl.ds(t, 1), :]
        return carry

    lax.fori_loop(0, SLOTS, body, 0, unroll=8)


def pack_kernel(targets, state, jacobian, holes, target_row, out, own):
    v = pl.program_id(0)
    free = jnp.where(v == 0, FREE[0], jnp.where(v == 1, FREE[1], jnp.where(v == 4, FREE[4], 0.0))).astype(f32)
    for r in range(R):
        for h in range(2):
            turned = state[0, r, h * L : (h + 1) * L, :].T
            hole = holes[2 * r + h : 2 * r + h + 1, :] == 0
            out[pl.ds(h * H + v * R + r, L, stride=C), :] = jnp.where(hole, free, turned)

    @pl.when(v == 0)
    def _():
        def body(k, carry):
            own[pl.ds(k, 1), :] = jacobian[pl.ds(targets[k], 1), :]
            return carry

        lax.fori_loop(0, SLOTS, body, 0, unroll=8)
        out[pl.ds(EXTRA[6], L, stride=C), :] = own[...].T
        out[pl.ds(EXTRA[7], L, stride=C), :] = jnp.broadcast_to(target_row[...], (L, L))
        for e in range(6):
            out[pl.ds(EXTRA[e], L, stride=C), :] = jnp.zeros((L, L), f32)


def donors_kernel(donated, packed, out, turned, sems):
    copies = []
    for e in range(V + 1):
        turned[e] = donated[e * SLOTS : (e + 1) * SLOTS, :].T
        copies.append(pltpu.make_async_copy(turned.at[e], out.at[:, EXTRA[e], :], sems.at[e]))
        copies[-1].start()
    for copy in copies:
        copy.wait()


def split(value):
    high = value.astype(bf16)
    return high, (value - high.astype(f32)).astype(bf16)


def dot(a, b):
    return jnp.dot(a, b, preferred_element_type=f32)


def plane_kernel(recv, da, dbt, fa, fbt, out, prep, left, column, field, ah, al, bh, bl):
    for cc in range(2):
        def rows(e):
            return recv[pl.ds(cc * C + EXTRA[e], N, stride=2 * C), :]

        def swapped(e):
            turned = rows(e).T
            return jnp.concatenate([turned[:N], turned[N:]], axis=1)

        weight = swapped(V)
        weight = weight / (weight + rows(6))
        target = rows(7).astype(i32)
        if cc == 0:
            column[...] = target & (B - 1)
        target = target >> 8
        for v in range(V + 1):
            value = weight if v == V else weight * swapped(v)
            for r in range(R):
                left[pl.ds(cc * H + v * R + r, N, stride=2 * H), :] = jnp.where(target == r, value, 0.0)

    places = lax.broadcasted_iota(i32, (B, SLOTS), 0)

    def scatter(s, carry):
        high, low = split(left[pl.ds(pl.multiple_of(s * 2 * H, 8), 2 * H), :])
        hit = (places == column[pl.ds(s, 1), :]).astype(f32).astype(bf16)
        spread = lax.dot_general(
            jnp.concatenate([high, low], axis=0), hit, (((1,), (1,)), ((), ())), preferred_element_type=f32
        )
        spread = spread[: 2 * H] + spread[2 * H :]
        for cc in range(2):
            for h in range(2):
                at = pl.ds(pl.multiple_of(s * 2 * C + cc * C + h * H, 8), H)
                part = spread[cc * H : (cc + 1) * H, h * L : (h + 1) * L]
                w = part[V * R :]
                prep[at, :] = part + (1.0 - jnp.concatenate([w] * 6, axis=0)) * recv[at, :]
        return carry

    lax.fori_loop(0, N, scatter, 0, unroll=2)

    da_h, da_l = split(da[...])
    db_h, db_l = split(dbt[...])
    fa_h, fa_l = split(fa[...])
    fb_h, fb_l = split(fbt[...])
    da_cat = jnp.concatenate([da_h, da_h, da_l], axis=1)
    fa_cat = jnp.concatenate([fa_h, fa_h, fa_l], axis=1)
    db_cat = jnp.concatenate([db_h, db_h, db_l], axis=0)
    fb_cat = jnp.concatenate([fb_h, fb_h, fb_l], axis=0)

    for cc in range(2):
        for r in range(R):
            for h in range(2):
                u = [prep[pl.ds(cc * C + h * H + v * R + r, N, stride=2 * C), :] for v in range(V)]
                rows_at, cols_at = slice(r * N, (r + 1) * N), slice(h * L, (h + 1) * L)
                inverse = 1.0 / u[0]
                va, vb = u[1] * inverse, u[2] * inverse
                pressure = 0.4 * (u[4] - 0.5 * (u[1] * u[1] + u[2] * u[2] + u[3] * u[3]) * inverse)
                total = u[4] + pressure
                flux_a = [u[1], u[1] * va + pressure, u[2] * va, u[3] * va, total * va]
                flux_b = [u[2], u[1] * vb, u[2] * vb + pressure, u[3] * vb, total * vb]
                for v in range(V):
                    field[v, rows_at, cols_at] = u[v]
                    ah[v, rows_at, cols_at], al[v, rows_at, cols_at] = split(flux_a[v])
                    bh[v, rows_at, cols_at], bl[v, rows_at, cols_at] = split(flux_b[v])

        def advance(v, carry):
            a1, a2, b1, b2 = ah[v], al[v], bh[v], bl[v]
            slope = dot(
                jnp.concatenate([da_cat, b1, b2, b1], axis=1),
                jnp.concatenate([a1, a2, a1, db_cat], axis=0),
            )
            s1, s2 = split(field[v] - section_weight * slope)
            smooth = dot(jnp.concatenate([s1, s2, s1], axis=1), fb_cat)
            s1, s2 = split(smooth)
            smooth = dot(fa_cat, jnp.concatenate([s1, s2, s1], axis=0))
            for r in range(R):
                for h in range(2):
                    out[pl.ds(cc * Q + h * V * R + v * R + r, N, stride=2 * Q), :] = smooth[
                        r * N : (r + 1) * N, h * L : (h + 1) * L
                    ]
            return carry

        lax.fori_loop(0, V, advance, 0)


def unpack_kernel(lines, out):
    v = pl.program_id(0)
    for r in range(R):
        for h in range(2):
            out[0, r, h * L : (h + 1) * L, :] = lines[pl.ds(h * V * R + v * R + r, L, stride=Q), :].T


def gather_donors(slots, state, jacobian):
    return pl.pallas_call(
        gather_kernel,
        out_shape=jax.ShapeDtypeStruct(((V + 1) * SLOTS, L), f32),
        in_specs=[SMEM, VMEM, VMEM],
        out_specs=VMEM,
        compiler_params=params(16),
        cost_estimate=cost(4_000_000),
        name="gather_donors",
    )(slots, state.reshape(V * R * B, L), jacobian.reshape(R * B, L))


def pack(targets, state, jacobian, holes, target_row):
    whole = lambda *shape: pl.BlockSpec(shape, lambda v: (0,) * len(shape))
    return pl.pallas_call(
        pack_kernel,
        grid=(V,),
        out_shape=jax.ShapeDtypeStruct((L * C, L), f32),
        in_specs=[
            SMEM,
            pl.BlockSpec((1, R, B, L), lambda v: (v, 0, 0, 0)),
            whole(R * B, L),
            whole(2 * R, L),
            whole(1, L),
        ],
        out_specs=whole(L * C, L),
        scratch_shapes=[pltpu.VMEM((SLOTS, L), f32)],
        compiler_params=params(24),
        cost_estimate=cost(8_000_000),
        name="pack",
    )(targets, state, jacobian.reshape(R * B, L), holes, target_row)


def add_donors(donated, packed):
    return pl.pallas_call(
        donors_kernel,
        out_shape=jax.ShapeDtypeStruct((L, C, L), f32),
        in_specs=[VMEM, ANY],
        out_specs=ANY,
        scratch_shapes=[pltpu.VMEM((V + 1, L, SLOTS), f32), pltpu.SemaphoreType.DMA((V + 1,))],
        input_output_aliases={1: 0},
        compiler_params=params(8),
        cost_estimate=cost(1_000_000),
        name="add_donors",
    )(donated, packed.reshape(L, C, L))


def planes(recv, da, dbt, fa, fbt):
    return pl.pallas_call(
        plane_kernel,
        out_shape=jax.ShapeDtypeStruct((L * Q, L), f32),
        in_specs=[VMEM] * 5,
        out_specs=VMEM,
        scratch_shapes=[
            pltpu.VMEM((L * C, L), f32),
            pltpu.VMEM((N * 2 * H, SLOTS), f32),
            pltpu.VMEM((N, SLOTS), i32),
            pltpu.VMEM((V, B, B), f32),
        ]
        + [pltpu.VMEM((V, B, B), bf16)] * 4,
        compiler_params=params(40),
        cost_estimate=cost(8_000_000, 8_000_000_000),
        name="planes",
    )(recv, da, dbt, fa, fbt)


def unpack(lines):
    return pl.pallas_call(
        unpack_kernel,
        grid=(V,),
        out_shape=jax.ShapeDtypeStruct((V, R, B, L), f32),
        in_specs=[pl.BlockSpec((L * Q, L), lambda v: (0, 0))],
        out_specs=pl.BlockSpec((1, R, B, L), lambda v: (v, 0, 0, 0)),
        compiler_params=params(24),
        cost_estimate=cost(6_000_000),
        name="unpack",
    )(lines)


def by_slot(blocks):
    return blocks.reshape(N, 2).T.reshape(SLOTS)


def turned_rows(matrix):
    return matrix.reshape(N, R, N, R).transpose(1, 0, 3, 2).reshape(B, B)


def exchange(value):
    return lax.all_to_all(value, "slab", split_axis=0, concat_axis=0, tiled=True)


def local(state, jacobian, iblank, donor_blocks, recv_blocks, deriv_a, deriv_b, filter_a, filter_b):
    state, jacobian = state[0], jacobian[0]
    donors = gather_donors(by_slot(donor_blocks[0]), state, jacobian)
    donated = lax.ppermute(donors, "grid", [(i, i ^ 1) for i in range(lax.axis_size("grid"))])
    flags = iblank[0].reshape(2 * R, L)
    targets = by_slot(recv_blocks[0])
    live = flags.reshape(-1)[targets] == 2
    target_row = jnp.where(live, targets, -1).astype(f32)[None]
    packed = pack(targets, state, jacobian, flags, target_row)
    sending = add_donors(donated, packed)
    recv = exchange(sending.reshape(N, 2 * C, L)).reshape(L * C, L)
    lines = planes(recv, turned_rows(deriv_a[0]), deriv_b[0].T, turned_rows(filter_a[0]), filter_b[0].T)
    result = exchange(lines.reshape(N, 2 * Q, L)).reshape(L * Q, L)
    return unpack(result)[None]


def solution(mesh):
    placed = (
        P("grid", None, "slab", None, None),
        P("grid", "slab", None, None),
        P("grid", "slab", None, None),
        P("grid", "slab", None),
        P("grid", "slab", None),
        P("grid", None, None),
        P("grid", None, None),
        P("grid", None, None),
        P("grid", None, None),
    )
    return jax.shard_map(
        local,
        mesh=mesh,
        in_specs=placed,
        out_specs=P("grid", None, "slab", None, None),
        check_vma=False,
    )
```

```python
import jax
import jax.numpy as jnp
from jax import lax
from jax.experimental import pallas as pl
from jax.experimental.pallas import tpu as pltpu
from jax.sharding import Mesh
from jax.sharding import PartitionSpec as P

V = 5
R = 4
N = 64
B = 256
L = 128
T = 2 * R
C = (V + 1) * T
Q = V * T
SLOTS = 128
EXTRA = Q
FREE = (1.0, 0.5, 0.0, 0.0, 2.5)

section_weight = 0.3
f32, bf16, i32 = jnp.float32, jnp.bfloat16, jnp.int32
VMEM = pl.BlockSpec(memory_space=pltpu.VMEM)
SMEM = pl.BlockSpec(memory_space=pltpu.SMEM)
HBM = pl.BlockSpec(memory_space=pltpu.HBM)


def params(mib):
    return pltpu.CompilerParams(vmem_limit_bytes=mib * 2**20)


def cost(nbytes, flops=0):
    return pl.CostEstimate(flops=flops, bytes_accessed=nbytes, transcendentals=0)


def pack_kernel(donors, targets, flags, holes, state, jacobian, sent, donor, target, flag, hole, u, jac, rows, out, sems):
    pairs = [(donors, donor), (targets, target), (flags, flag), (holes, hole), (jacobian, jac)]
    pairs += [(state.at[pl.ds(v * R * B, R * B)], u.at[pl.ds(v * R * B, R * B)]) for v in range(V)]
    fetch = [pltpu.make_async_copy(a, b, sems.at[i]) for i, (a, b) in enumerate(pairs)]
    for copy in fetch[3:] + fetch[:3]:
        copy.start()
    fetch[3].wait()
    lines_out = out.reshape(L, C, L)

    def send(v):
        at = pl.ds(v * T, T)
        copy = pltpu.make_async_copy(lines_out.at[:, at, :], sent.at[:, at, :], sems.at[V + 5 + v])
        copy.start()
        return copy

    sends = []
    for v in range(V):
        fetch[5 + v].wait()
        for r in range(R):
            for h in range(2):
                turned = u[(v * R + r) * B + h * L : (v * R + r) * B + (h + 1) * L, :].T
                out[pl.ds(v * T + h * R + r, L, stride=C), :] = jnp.where(
                    hole[2 * r + h : 2 * r + h + 1, :] == 0, FREE[v], turned
                )
        sends.append(send(v))
    for i in (0, 1, 2, 4):
        fetch[i].wait()
    lanes = lax.broadcasted_iota(i32, (1, SLOTS), 1)

    def body(s, row):
        for kk in range(2):
            k = kk * N + s
            t = donor[kk, s]
            rows[pl.ds(k, V, stride=SLOTS), :] = u[pl.ds(t, V, stride=R * B), :]
            rows[pl.ds(V * SLOTS + k, 1), :] = jac[pl.ds(t, 1), :]
            t = target[kk, s]
            rows[pl.ds((V + 1) * SLOTS + k, 1), :] = jac[pl.ds(t, 1), :]
            row = jnp.where(lanes == k, jnp.where(flag[t] == 2, t, -1), row)
        return row

    row = lax.fori_loop(0, N, body, jnp.full((1, SLOTS), -1, i32), unroll=8)
    for e in range(V + 2):
        out[pl.ds(EXTRA + e, L, stride=C), :] = rows[e * SLOTS : (e + 1) * SLOTS, :].T
    out[pl.ds(EXTRA + V + 2, L, stride=C), :] = jnp.broadcast_to(row.astype(f32), (L, SLOTS))
    sends.append(send(V))
    for copy in sends:
        copy.wait()


def matrix_kernel(da, db, fa, fb, out, rows):
    for at, matrix in ((0, da), (2, fa)):
        turned = matrix[...]
        for _ in range(2):
            for h in range(2):
                rows[h] = turned[:, h * L : (h + 1) * L]
            sorted_rows = [
                jnp.concatenate([rows[h, pl.ds(r, N, stride=R), :] for h in range(2)], axis=1) for r in range(R)
            ]
            turned = jnp.concatenate(sorted_rows, axis=0).T
        out[at] = turned
    out[1] = db[...].T
    out[3] = fb[...].T


def split(value):
    high = value.astype(bf16)
    return high, (value - high.astype(f32)).astype(bf16)


def dot(a, b):
    return jnp.dot(a, b, preferred_element_type=f32)


def plane_kernel(half, recv, mine, theirs, out, prep, left, column, field, ah, al, bh, bl, here, sems):
    fetch = [pltpu.make_async_copy(mine, here.at[0], sems.at[0]), pltpu.make_async_copy(theirs, here.at[1], sems.at[1])]
    for copy in fetch:
        copy.start()

    for g in range(2):
        def rows(grid, e):
            return recv[pl.ds(grid * N * C + EXTRA + e, N, stride=C), :]

        def swapped(e):
            turned = rows(1 - g, e).T
            return jnp.concatenate([turned[:N], turned[N:]], axis=1)

        weight = swapped(V)
        weight = weight / (weight + rows(g, V + 1))
        target = rows(g, V + 2).astype(i32)
        column[g * N : (g + 1) * N] = target & (L - 1)
        target = target >> 7
        for v in range(V + 1):
            value = weight if v == V else weight * swapped(v)
            for h in range(2):
                for r in range(R):
                    left[pl.ds(g * N * C + v * T + h * R + r, N, stride=C), :] = jnp.where(
                        target == 2 * r + h, value, 0.0
                    )

    places = lax.broadcasted_iota(i32, (L, SLOTS), 0)

    def scatter(s, carry):
        at = pl.multiple_of(s * C, 8)
        high, low = split(left[pl.ds(at, C), :])
        hit = (places == column[pl.ds(s, 1), :]).astype(f32).astype(bf16)
        spread = lax.dot_general(
            jnp.concatenate([high, low], axis=0), hit, (((1,), (1,)), ((), ())), preferred_element_type=f32
        )
        spread = spread[:C] + spread[C:]
        keep = 1.0 - spread[Q:]
        for v in range(V):
            prep[pl.ds(at + v * T, T), :] = spread[v * T : (v + 1) * T] + keep * recv[pl.ds(at + v * T, T), :]
        return carry

    lax.fori_loop(0, 2 * N, scatter, 0, unroll=64)
    for copy in fetch:
        copy.wait()

    for own in range(2):
        grid = jnp.bitwise_xor(half[0], own)
        da_h, da_l = split(here[own, 0])
        db_h, db_l = split(here[own, 1])
        fa_h, fa_l = split(here[own, 2])
        fb_h, fb_l = split(here[own, 3])
        for r in range(R):
            for h in range(2):
                u = [prep[pl.ds(grid * (N * C) + v * T + h * R + r, N, stride=C), :] for v in range(V)]
                cols = slice(h * L, (h + 1) * L)
                inverse = 1.0 / u[0]
                va, vb = u[1] * inverse, u[2] * inverse
                pressure = 0.4 * (u[4] - 0.5 * (u[1] * u[1] + u[2] * u[2] + u[3] * u[3]) * inverse)
                total = u[4] + pressure
                flux_a = [u[1], u[1] * va + pressure, u[2] * va, u[3] * va, total * va]
                flux_b = [u[2], u[1] * vb, u[2] * vb + pressure, u[3] * vb, total * vb]
                for v in range(V):
                    at = slice(v * B + r * N, v * B + (r + 1) * N)
                    field[at, cols] = u[v]
                    ah[at, cols], al[at, cols] = split(flux_a[v])
                    bh[at, cols], bl[at, cols] = split(flux_b[v])

        planes_at = [slice(v * B, (v + 1) * B) for v in range(V)]
        for at in planes_at:
            slope = dot(da_h, ah[at]) + dot(da_h, al[at]) + dot(da_l, ah[at])
            slope += dot(bh[at], db_h) + dot(bl[at], db_h) + dot(bh[at], db_l)
            ah[at], al[at] = split(field[at] - section_weight * slope)
        for at in planes_at:
            smooth = dot(ah[at], fb_h) + dot(al[at], fb_h) + dot(ah[at], fb_l)
            bh[at], bl[at] = split(smooth)
        for v, at in enumerate(planes_at):
            smooth = dot(fa_h, bh[at]) + dot(fa_h, bl[at]) + dot(fa_l, bh[at])
            for r in range(R):
                for h in range(2):
                    out[pl.ds(grid * (N * Q) + v * T + h * R + r, N, stride=Q), :] = smooth[
                        r * N : (r + 1) * N, h * L : (h + 1) * L
                    ]


def unpack_kernel(lines, result, out, sems):
    copies = []
    for v in range(V):
        for r in range(R):
            for h in range(2):
                out[v, r, h * L : (h + 1) * L, :] = lines[pl.ds(v * T + h * R + r, L, stride=Q), :].T
        copies.append(pltpu.make_async_copy(out.at[v], result.at[v], sems.at[v]))
        copies[-1].start()
    for copy in copies:
        copy.wait()


def pack(donors, targets, flags, state, jacobian):
    return pl.pallas_call(
        pack_kernel,
        out_shape=jax.ShapeDtypeStruct((L, C, L), f32),
        in_specs=[HBM] * 6,
        out_specs=HBM,
        scratch_shapes=[
            pltpu.SMEM((2, N), i32),
            pltpu.SMEM((2, N), i32),
            pltpu.SMEM((R * B,), i32),
            pltpu.VMEM((T, L), i32),
            pltpu.VMEM((V * R * B, L), f32),
            pltpu.VMEM((R * B, L), f32),
            pltpu.VMEM(((V + 2) * SLOTS, L), f32),
            pltpu.VMEM((L * C, L), f32),
            pltpu.SemaphoreType.DMA((2 * V + 6,)),
        ],
        compiler_params=params(58),
        cost_estimate=cost(8_000_000),
        name="pack",
    )(
        donors.T,
        targets.T,
        flags.reshape(R * B),
        flags.reshape(T, L),
        state.reshape(V * R * B, L),
        jacobian.reshape(R * B, L),
    )


def matrices(*given):
    return pl.pallas_call(
        matrix_kernel,
        out_shape=jax.ShapeDtypeStruct((4, B, B), f32),
        in_specs=[VMEM] * 4,
        out_specs=VMEM,
        scratch_shapes=[pltpu.VMEM((2, B, L), f32)],
        compiler_params=params(8),
        cost_estimate=cost(2_000_000),
        name="matrices",
    )(*given)


def planes(half, recv, mine, theirs):
    return pl.pallas_call(
        plane_kernel,
        out_shape=jax.ShapeDtypeStruct((L * Q, L), f32),
        in_specs=[SMEM, VMEM, HBM, HBM],
        out_specs=VMEM,
        scratch_shapes=[
            pltpu.VMEM((L * C, L), f32),
            pltpu.VMEM((L * C, SLOTS), f32),
            pltpu.VMEM((L, SLOTS), i32),
            pltpu.VMEM((V * B, B), f32),
        ]
        + [pltpu.VMEM((V * B, B), bf16)] * 4
        + [pltpu.VMEM((2, 4, B, B), f32), pltpu.SemaphoreType.DMA((2,))],
        compiler_params=params(40),
        cost_estimate=cost(8_000_000, 8_000_000_000),
        name="planes",
    )(half, recv, mine, theirs)


def unpack(lines):
    return pl.pallas_call(
        unpack_kernel,
        out_shape=jax.ShapeDtypeStruct((V, R, B, L), f32),
        in_specs=[VMEM],
        out_specs=HBM,
        scratch_shapes=[pltpu.VMEM((V, R, B, L), f32), pltpu.SemaphoreType.DMA((V,))],
        compiler_params=params(24),
        cost_estimate=cost(6_000_000),
        name="unpack",
    )(lines)


def exchange(value):
    return lax.all_to_all(value, ("half", "slab"), split_axis=0, concat_axis=0, tiled=True)


def local(state, jacobian, iblank, donor_blocks, recv_blocks, deriv_a, deriv_b, filter_a, filter_b):
    packed = pack(donor_blocks[0], recv_blocks[0], iblank[0], state[0], jacobian[0])
    recv = exchange(packed).reshape(L * C, L)
    mine = matrices(deriv_a[0], deriv_b[0], filter_a[0], filter_b[0])
    theirs = lax.ppermute(mine, "half", [(0, 1), (1, 0)])
    half = lax.axis_index("half").astype(i32)[None]
    lines = planes(half, recv, mine, theirs)
    result = exchange(lines.reshape(L, Q, L)).reshape(L * Q, L)
    return unpack(result)[None]


def solution(mesh):
    pairs = Mesh(mesh.devices.reshape(-1, 2, N), ("pair", "half", "slab"))
    grid = ("pair", "half")
    placed = (
        P(grid, None, "slab", None, None),
        P(grid, "slab", None, None),
        P(grid, "slab", None, None),
        P(grid, "slab", None),
        P(grid, "slab", None),
        P(grid, None, None),
        P(grid, None, None),
        P(grid, None, None),
        P(grid, None, None),
    )
    return jax.shard_map(
        local,
        mesh=pairs,
        in_specs=placed,
        out_specs=P(grid, None, "slab", None, None),
        check_vma=False,
    )
```

```python
import jax
import jax.numpy as jnp
from jax import lax
from jax.experimental import pallas as pl
from jax.experimental.pallas import tpu as pltpu
from jax.sharding import Mesh
from jax.sharding import PartitionSpec as P

V = 5
R = 4
N = 64
B = 256
L = 128
T = 2 * R
C = (V + 1) * T
Q = V * T
SLOTS = 128
NOWHERE = 4 * R * B
EXTRA = Q
FREE = (1.0, 0.5, 0.0, 0.0, 2.5)

section_weight = 0.3
f32, bf16, i32 = jnp.float32, jnp.bfloat16, jnp.int32
VMEM = pl.BlockSpec(memory_space=pltpu.VMEM)
SMEM = pl.BlockSpec(memory_space=pltpu.SMEM)
HBM = pl.BlockSpec(memory_space=pltpu.HBM)


def params(mib):
    return pltpu.CompilerParams(vmem_limit_bytes=mib * 2**20)


def cost(nbytes, flops=0):
    return pl.CostEstimate(flops=flops, bytes_accessed=nbytes, transcendentals=0)


def pack_kernel(donors, targets, flags, holes, state, jacobian, sent, donor, target, flag, hole, u, jac, rows, out, sems):
    pairs = [(donors, donor), (targets, target), (flags, flag), (holes, hole), (jacobian, jac)]
    pairs += [(state.at[pl.ds(v * R * B, R * B)], u.at[pl.ds(v * R * B, R * B)]) for v in range(V)]
    fetch = [pltpu.make_async_copy(a, b, sems.at[i]) for i, (a, b) in enumerate(pairs)]
    for copy in [fetch[3]] + fetch[5:] + [fetch[4]] + fetch[:3]:
        copy.start()
    fetch[3].wait()
    lines_out = out.reshape(L, C, L)

    def send(v):
        at = pl.ds(v * T, T)
        copy = pltpu.make_async_copy(lines_out.at[:, at, :], sent.at[:, at, :], sems.at[V + 5 + v])
        copy.start()
        return copy

    sends = []
    for v in range(V):
        fetch[5 + v].wait()
        for r in range(R):
            for h in range(2):
                turned = u[(v * R + r) * B + h * L : (v * R + r) * B + (h + 1) * L, :].T
                out[pl.ds(v * T + h * R + r, L, stride=C), :] = jnp.where(
                    hole[2 * r + h : 2 * r + h + 1, :] == 0, FREE[v], turned
                )
        sends.append(send(v))
    for i in (0, 1, 2, 4):
        fetch[i].wait()
    lanes = lax.broadcasted_iota(i32, (1, SLOTS), 1)

    def body(s, row):
        for kk in range(2):
            k = kk * N + s
            t = donor[kk, s]
            rows[pl.ds(k, V, stride=SLOTS), :] = u[pl.ds(t, V, stride=R * B), :]
            rows[pl.ds(V * SLOTS + k, 1), :] = jac[pl.ds(t, 1), :]
            t = target[kk, s]
            rows[pl.ds((V + 1) * SLOTS + k, 1), :] = jac[pl.ds(t, 1), :]
            row = jnp.where(lanes == k, jnp.where(flag[t] == 2, t, NOWHERE), row)
        return row

    row = lax.fori_loop(0, N, body, jnp.full((1, SLOTS), NOWHERE, i32), unroll=8)
    for e in range(V + 2):
        out[pl.ds(EXTRA + e, L, stride=C), :] = rows[e * SLOTS : (e + 1) * SLOTS, :].T
    out[pl.ds(EXTRA + V + 2, L, stride=C), :] = jnp.broadcast_to(row.astype(f32), (L, SLOTS))
    sends.append(send(V))
    for copy in sends:
        copy.wait()


def matrix_kernel(da, db, fa, fb, out, rows):
    for at, matrix in ((0, da), (2, fa)):
        turned = matrix[...]
        for _ in range(2):
            for h in range(2):
                rows[h] = turned[:, h * L : (h + 1) * L]
            sorted_rows = [
                jnp.concatenate([rows[h, pl.ds(r, N, stride=R), :] for h in range(2)], axis=1) for r in range(R)
            ]
            turned = jnp.concatenate(sorted_rows, axis=0).T
        out[at] = turned
    out[1] = db[...].T
    out[3] = fb[...].T


def split(value):
    high = value.astype(bf16)
    return high, (value - high.astype(f32)).astype(bf16)


def dot(a, b):
    return jnp.dot(a, b, preferred_element_type=f32)


def plane_kernel(half, recv, mine, theirs, out, prep, high, low, place, field, ah, al, bh, bl, here, sems):
    fetch = [pltpu.make_async_copy(mine, here.at[0], sems.at[0]), pltpu.make_async_copy(theirs, here.at[1], sems.at[1])]
    for copy in fetch:
        copy.start()

    for g in range(2):
        def rows(grid, e):
            return recv[pl.ds(grid * N * C + EXTRA + e, N, stride=C), :]

        def swapped(e):
            turned = rows(1 - g, e).T
            return jnp.concatenate([turned[:N], turned[N:]], axis=1)

        at = slice(g * N, (g + 1) * N)
        weight = swapped(V)
        weight = weight / (weight + rows(g, V + 1))
        place[at] = rows(g, V + 2).astype(i32)
        for v in range(V + 1):
            value = weight if v == V else weight * swapped(v)
            high[v, at] = value.astype(bf16).astype(f32)
            low[v, at] = value - high[v, at]

    places = lax.broadcasted_iota(i32, (L, SLOTS), 0)
    parts = lax.broadcasted_iota(i32, (T, SLOTS), 0)
    none = jnp.zeros((L, SLOTS), bf16)

    def masked(values, s, part):
        return jnp.concatenate([jnp.where(part, values[v, s : s + 1, :], 0.0) for v in range(V + 1)], axis=0)

    for s in range(0, 2 * N, 2):
        hits, values = [], []
        for i in range(2):
            target = place[s + i : s + i + 1, :]
            hits.append((places == (target & (L - 1))).astype(f32).astype(bf16))
            part = parts == ((target >> 8) + ((target >> 7) & 1) * R)
            values.append(jnp.concatenate([masked(x, s + i, part) for x in (high, low)], axis=0).astype(bf16))
        values = jnp.concatenate(values, axis=1)
        hits = [jnp.concatenate([hits[0], none], axis=1), jnp.concatenate([none, hits[1]], axis=1)]
        spread = lax.dot_general(
            values, jnp.concatenate(hits, axis=0), (((1,), (1,)), ((), ())), preferred_element_type=f32
        )
        spread = spread[:C] + spread[C:]
        keep = 1.0 - spread[Q:]
        for i in range(2):
            cols = slice(i * L, (i + 1) * L)
            for v in range(V):
                at = slice((s + i) * C + v * T, (s + i) * C + (v + 1) * T)
                prep[at, :] = spread[v * T : (v + 1) * T, cols] + keep[:, cols] * recv[at, :]

    for copy in fetch:
        copy.wait()

    for own in range(2):
        grid = jnp.bitwise_xor(half[0], own)
        da_h, da_l = split(here[own, 0])
        db_h, db_l = split(here[own, 1])
        fa_h, fa_l = split(here[own, 2])
        fb_h, fb_l = split(here[own, 3])
        for r in range(R):
            for h in range(2):
                u = [prep[pl.ds(grid * (N * C) + v * T + h * R + r, N, stride=C), :] for v in range(V)]
                cols = slice(h * L, (h + 1) * L)
                inverse = 1.0 / u[0]
                va, vb = u[1] * inverse, u[2] * inverse
                pressure = 0.4 * (u[4] - 0.5 * (u[1] * u[1] + u[2] * u[2] + u[3] * u[3]) * inverse)
                total = u[4] + pressure
                flux_a = [u[1], u[1] * va + pressure, u[2] * va, u[3] * va, total * va]
                flux_b = [u[2], u[1] * vb, u[2] * vb + pressure, u[3] * vb, total * vb]
                for v in range(V):
                    at = slice(v * B + r * N, v * B + (r + 1) * N)
                    field[at, cols] = u[v]
                    ah[at, cols], al[at, cols] = split(flux_a[v])
                    bh[at, cols], bl[at, cols] = split(flux_b[v])

        planes_at = [slice(v * B, (v + 1) * B) for v in range(V)]
        for at in planes_at:
            slope = dot(da_h, ah[at]) + dot(da_h, al[at]) + dot(da_l, ah[at])
            slope += dot(bh[at], db_h) + dot(bl[at], db_h) + dot(bh[at], db_l)
            ah[at], al[at] = split(field[at] - section_weight * slope)
        for at in planes_at:
            smooth = dot(ah[at], fb_h) + dot(al[at], fb_h) + dot(ah[at], fb_l)
            bh[at], bl[at] = split(smooth)
        for v, at in enumerate(planes_at):
            smooth = dot(fa_h, bh[at]) + dot(fa_h, bl[at]) + dot(fa_l, bh[at])
            for r in range(R):
                for h in range(2):
                    out[pl.ds(grid * (N * Q) + v * T + h * R + r, N, stride=Q), :] = smooth[
                        r * N : (r + 1) * N, h * L : (h + 1) * L
                    ]


def unpack_kernel(lines, result, out, sems):
    copies = []
    for v in range(V):
        for r in range(R):
            for h in range(2):
                out[v, r, h * L : (h + 1) * L, :] = lines[pl.ds(v * T + h * R + r, L, stride=Q), :].T
        copies.append(pltpu.make_async_copy(out.at[v], result.at[v], sems.at[v]))
        copies[-1].start()
    for copy in copies:
        copy.wait()


def pack(donors, targets, flags, state, jacobian):
    return pl.pallas_call(
        pack_kernel,
        out_shape=jax.ShapeDtypeStruct((L, C, L), f32),
        in_specs=[HBM] * 6,
        out_specs=HBM,
        scratch_shapes=[
            pltpu.SMEM((2, N), i32),
            pltpu.SMEM((2, N), i32),
            pltpu.SMEM((R * B,), i32),
            pltpu.VMEM((T, L), i32),
            pltpu.VMEM((V * R * B, L), f32),
            pltpu.VMEM((R * B, L), f32),
            pltpu.VMEM(((V + 2) * SLOTS, L), f32),
            pltpu.VMEM((L * C, L), f32),
            pltpu.SemaphoreType.DMA((2 * V + 6,)),
        ],
        compiler_params=params(58),
        cost_estimate=cost(8_000_000),
        name="pack",
    )(
        donors.T,
        targets.T,
        flags.reshape(R * B),
        flags.reshape(T, L),
        state.reshape(V * R * B, L),
        jacobian.reshape(R * B, L),
    )


def matrices(*given):
    return pl.pallas_call(
        matrix_kernel,
        out_shape=jax.ShapeDtypeStruct((4, B, B), f32),
        in_specs=[VMEM] * 4,
        out_specs=VMEM,
        scratch_shapes=[pltpu.VMEM((2, B, L), f32)],
        compiler_params=params(8),
        cost_estimate=cost(2_000_000),
        name="matrices",
    )(*given)


def planes(half, recv, mine, theirs):
    return pl.pallas_call(
        plane_kernel,
        out_shape=jax.ShapeDtypeStruct((L * Q, L), f32),
        in_specs=[SMEM, VMEM, HBM, HBM],
        out_specs=VMEM,
        scratch_shapes=[
            pltpu.VMEM((L * C, L), f32),
            pltpu.VMEM((V + 1, L, SLOTS), f32),
            pltpu.VMEM((V + 1, L, SLOTS), f32),
            pltpu.VMEM((L, SLOTS), i32),
            pltpu.VMEM((V * B, B), f32),
        ]
        + [pltpu.VMEM((V * B, B), bf16)] * 4
        + [pltpu.VMEM((2, 4, B, B), f32), pltpu.SemaphoreType.DMA((2,))],
        compiler_params=params(40),
        cost_estimate=cost(8_000_000, 8_000_000_000),
        name="planes",
    )(half, recv, mine, theirs)


def unpack(lines):
    return pl.pallas_call(
        unpack_kernel,
        out_shape=jax.ShapeDtypeStruct((V, R, B, L), f32),
        in_specs=[VMEM],
        out_specs=HBM,
        scratch_shapes=[pltpu.VMEM((V, R, B, L), f32), pltpu.SemaphoreType.DMA((V,))],
        compiler_params=params(24),
        cost_estimate=cost(6_000_000),
        name="unpack",
    )(lines)


def exchange(value):
    return lax.all_to_all(value, ("half", "slab"), split_axis=0, concat_axis=0, tiled=True)


def local(state, jacobian, iblank, donor_blocks, recv_blocks, deriv_a, deriv_b, filter_a, filter_b):
    packed = pack(donor_blocks[0], recv_blocks[0], iblank[0], state[0], jacobian[0])
    recv = exchange(packed).reshape(L * C, L)
    mine = matrices(deriv_a[0], deriv_b[0], filter_a[0], filter_b[0])
    theirs = lax.ppermute(mine, "half", [(0, 1), (1, 0)])
    half = lax.axis_index("half").astype(i32)[None]
    lines = planes(half, recv, mine, theirs)
    result = exchange(lines.reshape(L, Q, L)).reshape(L * Q, L)
    return unpack(result)[None]


def solution(mesh):
    pairs = Mesh(mesh.devices.reshape(-1, 2, N), ("pair", "half", "slab"))
    grid = ("pair", "half")
    placed = (
        P(grid, None, "slab", None, None),
        P(grid, "slab", None, None),
        P(grid, "slab", None, None),
        P(grid, "slab", None),
        P(grid, "slab", None),
        P(grid, None, None),
        P(grid, None, None),
        P(grid, None, None),
        P(grid, None, None),
    )
    return jax.shard_map(
        local,
        mesh=pairs,
        in_specs=placed,
        out_specs=P(grid, None, "slab", None, None),
        check_vma=False,
    )
```

```python
import jax
import jax.numpy as jnp
from jax import lax
from jax.experimental import pallas as pl
from jax.experimental.pallas import tpu as pltpu
from jax.sharding import Mesh
from jax.sharding import PartitionSpec as P

V = 5
R = 4
N = 64
B = 256
L = 128
T = 2 * R
C = (V + 1) * T
Q = V * T
SLOTS = 128
LEAD = 49
NOWHERE = 4 * R * B
EXTRA = Q
FREE = (1.0, 0.5, 0.0, 0.0, 2.5)

section_weight = 0.3
f32, bf16, i32 = jnp.float32, jnp.bfloat16, jnp.int32
VMEM = pl.BlockSpec(memory_space=pltpu.VMEM)
SMEM = pl.BlockSpec(memory_space=pltpu.SMEM)
HBM = pl.BlockSpec(memory_space=pltpu.HBM)


def params(mib):
    return pltpu.CompilerParams(vmem_limit_bytes=mib * 2**20)


def cost(nbytes, flops=0):
    return pl.CostEstimate(flops=flops, bytes_accessed=nbytes, transcendentals=0)


def pack_kernel(donors, targets, flags, holes, state, jacobian, sent, donor, target, flag, hole, u, jac, rows, out, sems):
    pairs = [(donors, donor), (targets, target), (flags, flag), (holes, hole), (jacobian, jac)]
    pairs += [(state.at[pl.ds(v * R * B, R * B)], u.at[pl.ds(v * R * B, R * B)]) for v in range(V)]
    fetch = [pltpu.make_async_copy(a, b, sems.at[i]) for i, (a, b) in enumerate(pairs)]
    for copy in [fetch[3]] + fetch[5:] + [fetch[4]] + fetch[:3]:
        copy.start()
    fetch[3].wait()
    lines_out = out.reshape(L, C, L)

    def send(v):
        at = pl.ds(v * T, T)
        copy = pltpu.make_async_copy(lines_out.at[:, at, :], sent.at[:, at, :], sems.at[V + 5 + v])
        copy.start()
        return copy

    sends = []
    for v in range(V):
        fetch[5 + v].wait()
        for r in range(R):
            for h in range(2):
                turned = u[(v * R + r) * B + h * L : (v * R + r) * B + (h + 1) * L, :].T
                out[pl.ds(v * T + h * R + r, L, stride=C), :] = jnp.where(
                    hole[2 * r + h : 2 * r + h + 1, :] == 0, FREE[v], turned
                )
        sends.append(send(v))
    for i in (0, 1, 2, 4):
        fetch[i].wait()
    lanes = lax.broadcasted_iota(i32, (1, SLOTS), 1)

    def body(s, row):
        for kk in range(2):
            k = kk * N + s
            t = donor[kk, s]
            rows[pl.ds(k, V, stride=SLOTS), :] = u[pl.ds(t, V, stride=R * B), :]
            rows[pl.ds(V * SLOTS + k, 1), :] = jac[pl.ds(t, 1), :]
            t = target[kk, s]
            rows[pl.ds((V + 1) * SLOTS + k, 1), :] = jac[pl.ds(t, 1), :]
            row = jnp.where(lanes == k, jnp.where(flag[t] == 2, t, NOWHERE), row)
        return row

    row = lax.fori_loop(0, N, body, jnp.full((1, SLOTS), NOWHERE, i32), unroll=8)
    for e in range(V + 2):
        out[pl.ds(EXTRA + e, L, stride=C), :] = rows[e * SLOTS : (e + 1) * SLOTS, :].T
    out[pl.ds(EXTRA + V + 2, L, stride=C), :] = jnp.broadcast_to(row.astype(f32), (L, SLOTS))
    sends.append(send(V))
    for copy in sends:
        copy.wait()


def matrix_kernel(da, db, fa, fb, out, rows):
    for at, matrix in ((0, da), (2, fa)):
        turned = matrix[...]
        for _ in range(2):
            for h in range(2):
                rows[h] = turned[:, h * L : (h + 1) * L]
            sorted_rows = [
                jnp.concatenate([rows[h, pl.ds(r, N, stride=R), :] for h in range(2)], axis=1) for r in range(R)
            ]
            turned = jnp.concatenate(sorted_rows, axis=0).T
        out[at] = turned
    out[1] = db[...].T
    out[3] = fb[...].T


def split(value):
    high = value.astype(bf16)
    return high, (value - high.astype(f32)).astype(bf16)


def dot(a, b):
    return jnp.dot(a, b, preferred_element_type=f32)


def plane_kernel(half, recv, mine, theirs, out, prep, high, low, place, field, ah, al, bh, bl, here, sems):
    fetch = [pltpu.make_async_copy(mine, here.at[0], sems.at[0]), pltpu.make_async_copy(theirs, here.at[1], sems.at[1])]
    for copy in fetch:
        copy.start()

    for g in range(2):
        def rows(grid, e):
            return recv[pl.ds(grid * N * C + EXTRA + e, N, stride=C), :]

        def swapped(e):
            turned = rows(1 - g, e).T
            return jnp.concatenate([turned[:N], turned[N:]], axis=1)

        at = slice(g * N, (g + 1) * N)
        weight = swapped(V)
        weight = weight / (weight + rows(g, V + 1))
        place[at] = rows(g, V + 2).astype(i32)
        for v in range(V + 1):
            value = weight if v == V else weight * swapped(v)
            high[v, at] = value.astype(bf16).astype(f32)
            low[v, at] = value - high[v, at]

    places = lax.broadcasted_iota(i32, (L, SLOTS), 0)
    parts = lax.broadcasted_iota(i32, (T, SLOTS), 0)
    none = jnp.zeros((L, SLOTS), bf16)

    def masked(values, s, part):
        return jnp.concatenate([jnp.where(part, values[v, s : s + 1, :], 0.0) for v in range(V + 1)], axis=0)

    def scatter(s):
        hits, values = [], []
        for i in range(2):
            target = place[s + i : s + i + 1, :]
            hits.append((places == (target & (L - 1))).astype(f32).astype(bf16))
            part = parts == ((target >> 8) + ((target >> 7) & 1) * R)
            values.append(jnp.concatenate([masked(x, s + i, part) for x in (high, low)], axis=0).astype(bf16))
        values = jnp.concatenate(values, axis=1)
        hits = [jnp.concatenate([hits[0], none], axis=1), jnp.concatenate([none, hits[1]], axis=1)]
        spread = lax.dot_general(
            values, jnp.concatenate(hits, axis=0), (((1,), (1,)), ((), ())), preferred_element_type=f32
        )
        spread = spread[:C] + spread[C:]
        keep = 1.0 - spread[Q:]
        for i in range(2):
            cols = slice(i * L, (i + 1) * L)
            for v in range(V):
                at = slice((s + i) * C + v * T, (s + i) * C + (v + 1) * T)
                prep[at, :] = spread[v * T : (v + 1) * T, cols] + keep[:, cols] * recv[at, :]

    def fluxes(g):
        for r in range(R):
            for h in range(2):
                u = [prep[pl.ds(g * N * C + v * T + h * R + r, N, stride=C), :] for v in range(V)]
                cols = slice(h * L, (h + 1) * L)
                inverse = 1.0 / u[0]
                va, vb = u[1] * inverse, u[2] * inverse
                pressure = 0.4 * (u[4] - 0.5 * (u[1] * u[1] + u[2] * u[2] + u[3] * u[3]) * inverse)
                total = u[4] + pressure
                flux_a = [u[1], u[1] * va + pressure, u[2] * va, u[3] * va, total * va]
                flux_b = [u[2], u[1] * vb, u[2] * vb + pressure, u[3] * vb, total * vb]
                for v in range(V):
                    at = slice((g * V + v) * B + r * N, (g * V + v) * B + (r + 1) * N)
                    field[at, cols] = u[v]
                    ah[at, cols], al[at, cols] = split(flux_a[v])
                    bh[at, cols], bl[at, cols] = split(flux_b[v])

    def products(g):
        own = jnp.bitwise_xor(half[0], g)
        (da_h, da_l), (db_h, db_l), (fa_h, fa_l), (fb_h, fb_l) = [split(here[own, m]) for m in range(4)]

        def section(v, at):
            slope = dot(da_h, ah[at]) + dot(da_h, al[at]) + dot(da_l, ah[at])
            slope += dot(bh[at], db_h) + dot(bl[at], db_h) + dot(bh[at], db_l)
            ah[at], al[at] = split(field[at] - section_weight * slope)

        def second(v, at):
            smooth = dot(ah[at], fb_h) + dot(al[at], fb_h) + dot(ah[at], fb_l)
            bh[at], bl[at] = split(smooth)

        def first(v, at):
            smooth = dot(fa_h, bh[at]) + dot(fa_h, bl[at]) + dot(fa_l, bh[at])
            for r in range(R):
                for h in range(2):
                    out[pl.ds(g * N * Q + v * T + h * R + r, N, stride=Q), :] = smooth[
                        r * N : (r + 1) * N, h * L : (h + 1) * L
                    ]

        return [
            (lambda stage=stage, v=v: stage(v, slice((g * V + v) * B, (g * V + v + 1) * B)))
            for stage in (section, second, first)
            for v in range(V)
        ]

    pairs = list(range(0, 2 * N, 2))
    later = pairs[LEAD:]
    for s in pairs[:LEAD]:
        scatter(s)
    for copy in fetch:
        copy.wait()
    fluxes(0)
    for step in products(0):
        for s in later[:1]:
            scatter(s)
        later = later[1:]
        step()
    for s in later:
        scatter(s)
    fluxes(1)
    for step in products(1):
        step()


def unpack_kernel(lines, result, out, sems):
    copies = []
    for v in range(V):
        for r in range(R):
            for h in range(2):
                out[v, r, h * L : (h + 1) * L, :] = lines[pl.ds(v * T + h * R + r, L, stride=Q), :].T
        copies.append(pltpu.make_async_copy(out.at[v], result.at[v], sems.at[v]))
        copies[-1].start()
    for copy in copies:
        copy.wait()


def pack(donors, targets, flags, state, jacobian):
    return pl.pallas_call(
        pack_kernel,
        out_shape=jax.ShapeDtypeStruct((L, C, L), f32),
        in_specs=[HBM] * 6,
        out_specs=HBM,
        scratch_shapes=[
            pltpu.SMEM((2, N), i32),
            pltpu.SMEM((2, N), i32),
            pltpu.SMEM((R * B,), i32),
            pltpu.VMEM((T, L), i32),
            pltpu.VMEM((V * R * B, L), f32),
            pltpu.VMEM((R * B, L), f32),
            pltpu.VMEM(((V + 2) * SLOTS, L), f32),
            pltpu.VMEM((L * C, L), f32),
            pltpu.SemaphoreType.DMA((2 * V + 6,)),
        ],
        compiler_params=params(58),
        cost_estimate=cost(8_000_000),
        name="pack",
    )(
        donors.T,
        targets.T,
        flags.reshape(R * B),
        flags.reshape(T, L),
        state.reshape(V * R * B, L),
        jacobian.reshape(R * B, L),
    )


def matrices(*given):
    return pl.pallas_call(
        matrix_kernel,
        out_shape=jax.ShapeDtypeStruct((4, B, B), f32),
        in_specs=[VMEM] * 4,
        out_specs=VMEM,
        scratch_shapes=[pltpu.VMEM((2, B, L), f32)],
        compiler_params=params(8),
        cost_estimate=cost(2_000_000),
        name="matrices",
    )(*given)


def planes(half, recv, mine, theirs):
    return pl.pallas_call(
        plane_kernel,
        out_shape=jax.ShapeDtypeStruct((L * Q, L), f32),
        in_specs=[SMEM, VMEM, HBM, HBM],
        out_specs=VMEM,
        scratch_shapes=[
            pltpu.VMEM((L * C, L), f32),
            pltpu.VMEM((V + 1, L, SLOTS), f32),
            pltpu.VMEM((V + 1, L, SLOTS), f32),
            pltpu.VMEM((L, SLOTS), i32),
            pltpu.VMEM((2 * V * B, B), f32),
        ]
        + [pltpu.VMEM((2 * V * B, B), bf16)] * 4
        + [pltpu.VMEM((2, 4, B, B), f32), pltpu.SemaphoreType.DMA((2,))],
        compiler_params=params(40),
        cost_estimate=cost(8_000_000, 8_000_000_000),
        name="planes",
    )(half, recv, mine, theirs)


def unpack(lines):
    return pl.pallas_call(
        unpack_kernel,
        out_shape=jax.ShapeDtypeStruct((V, R, B, L), f32),
        in_specs=[VMEM],
        out_specs=HBM,
        scratch_shapes=[pltpu.VMEM((V, R, B, L), f32), pltpu.SemaphoreType.DMA((V,))],
        compiler_params=params(24),
        cost_estimate=cost(6_000_000),
        name="unpack",
    )(lines)


def exchange(value):
    return lax.all_to_all(value, ("half", "slab"), split_axis=0, concat_axis=0, tiled=True)


def local(state, jacobian, iblank, donor_blocks, recv_blocks, deriv_a, deriv_b, filter_a, filter_b):
    packed = pack(donor_blocks[0], recv_blocks[0], iblank[0], state[0], jacobian[0])
    recv = exchange(packed).reshape(L * C, L)
    mine = matrices(deriv_a[0], deriv_b[0], filter_a[0], filter_b[0])
    theirs = lax.ppermute(mine, "half", [(0, 1), (1, 0)])
    half = lax.axis_index("half").astype(i32)[None]
    lines = planes(half, recv, mine, theirs)
    result = exchange(lines.reshape(L, Q, L)).reshape(L * Q, L)
    return unpack(result)[None]


def solution(mesh):
    pairs = Mesh(mesh.devices.reshape(-1, 2, N), ("pair", "half", "slab"))
    grid = ("pair", "half")
    placed = (
        P(grid, None, "slab", None, None),
        P(grid, "slab", None, None),
        P(grid, "slab", None, None),
        P(grid, "slab", None),
        P(grid, "slab", None),
        P(grid, None, None),
        P(grid, None, None),
        P(grid, None, None),
        P(grid, None, None),
    )
    return jax.shard_map(
        local,
        mesh=pairs,
        in_specs=placed,
        out_specs=P(grid, None, "slab", None, None),
        check_vma=False,
    )
```

```python
import jax
import jax.numpy as jnp
from jax import lax
from jax.experimental import pallas as pl
from jax.experimental.pallas import tpu as pltpu
from jax.sharding import Mesh
from jax.sharding import PartitionSpec as P

V = 5
R = 4
N = 64
B = 256
L = 128
T = 2 * R
C = (V + 1) * T
Q = V * T
SLOTS = 128
LEAD = 34
AHEAD = 2
NOWHERE = 4 * R * B
EXTRA = Q
FREE = (1.0, 0.5, 0.0, 0.0, 2.5)

section_weight = 0.3
f32, bf16, i32 = jnp.float32, jnp.bfloat16, jnp.int32
VMEM = pl.BlockSpec(memory_space=pltpu.VMEM)
SMEM = pl.BlockSpec(memory_space=pltpu.SMEM)
HBM = pl.BlockSpec(memory_space=pltpu.HBM)


def params(mib):
    return pltpu.CompilerParams(vmem_limit_bytes=mib * 2**20)


def cost(nbytes, flops=0):
    return pl.CostEstimate(flops=flops, bytes_accessed=nbytes, transcendentals=0)


def pack_kernel(donors, targets, flags, holes, state, jacobian, sent, donor, target, flag, hole, u, jac, rows, out, sems):
    pairs = [(donors, donor), (targets, target), (flags, flag), (holes, hole), (jacobian, jac)]
    pairs += [(state.at[pl.ds(v * R * B, R * B)], u.at[pl.ds(v * R * B, R * B)]) for v in range(V)]
    fetch = [pltpu.make_async_copy(a, b, sems.at[i]) for i, (a, b) in enumerate(pairs)]
    for copy in [fetch[3]] + fetch[5:] + [fetch[4]] + fetch[:3]:
        copy.start()
    fetch[3].wait()
    lines_out = out.reshape(L, C, L)

    def send(v):
        at = pl.ds(v * T, T)
        copy = pltpu.make_async_copy(lines_out.at[:, at, :], sent.at[:, at, :], sems.at[V + 5 + v])
        copy.start()
        return copy

    sends = []
    for v in range(V):
        fetch[5 + v].wait()
        for r in range(R):
            for h in range(2):
                turned = u[(v * R + r) * B + h * L : (v * R + r) * B + (h + 1) * L, :].T
                out[pl.ds(v * T + h * R + r, L, stride=C), :] = jnp.where(
                    hole[2 * r + h : 2 * r + h + 1, :] == 0, FREE[v], turned
                )
        sends.append(send(v))
    for i in (0, 1, 2, 4):
        fetch[i].wait()
    lanes = lax.broadcasted_iota(i32, (1, SLOTS), 1)

    def body(s, row):
        for kk in range(2):
            k = kk * N + s
            t = donor[kk, s]
            rows[pl.ds(k, V, stride=SLOTS), :] = u[pl.ds(t, V, stride=R * B), :]
            rows[pl.ds(V * SLOTS + k, 1), :] = jac[pl.ds(t, 1), :]
            t = target[kk, s]
            rows[pl.ds((V + 1) * SLOTS + k, 1), :] = jac[pl.ds(t, 1), :]
            row = jnp.where(lanes == k, jnp.where(flag[t] == 2, t, NOWHERE), row)
        return row

    row = lax.fori_loop(0, N, body, jnp.full((1, SLOTS), NOWHERE, i32), unroll=8)
    for e in range(V + 2):
        out[pl.ds(EXTRA + e, L, stride=C), :] = rows[e * SLOTS : (e + 1) * SLOTS, :].T
    out[pl.ds(EXTRA + V + 2, L, stride=C), :] = jnp.broadcast_to(row.astype(f32), (L, SLOTS))
    sends.append(send(V))
    for copy in sends:
        copy.wait()


def matrix_kernel(da, db, fa, fb, out, rows):
    for at, matrix in ((0, da), (2, fa)):
        turned = matrix[...]
        for _ in range(2):
            for h in range(2):
                rows[h] = turned[:, h * L : (h + 1) * L]
            sorted_rows = [
                jnp.concatenate([rows[h, pl.ds(r, N, stride=R), :] for h in range(2)], axis=1) for r in range(R)
            ]
            turned = jnp.concatenate(sorted_rows, axis=0).T
        out[at] = turned
    out[1] = db[...].T
    out[3] = fb[...].T


def split(value):
    high = value.astype(bf16)
    return high, (value - high.astype(f32)).astype(bf16)


def dot(a, b):
    return jnp.dot(a, b, preferred_element_type=f32)


def plane_kernel(half, recv, mine, theirs, out, prep, high, low, place, field, ah, al, bh, bl, here, sems):
    fetch = [pltpu.make_async_copy(mine, here.at[0], sems.at[0]), pltpu.make_async_copy(theirs, here.at[1], sems.at[1])]
    for own in range(2):
        @pl.when(half[0] == own)
        def _(own=own):
            fetch[own].start()
            fetch[1 - own].start()

    for g in range(2):
        def rows(grid, e):
            return recv[pl.ds(grid * N * C + EXTRA + e, N, stride=C), :]

        def swapped(e):
            turned = rows(1 - g, e).T
            return jnp.concatenate([turned[:N], turned[N:]], axis=1)

        at = slice(g * N, (g + 1) * N)
        weight = swapped(V)
        weight = weight / (weight + rows(g, V + 1))
        place[at] = rows(g, V + 2).astype(i32)
        for v in range(V + 1):
            value = weight if v == V else weight * swapped(v)
            high[v, at] = value.astype(bf16).astype(f32)
            low[v, at] = value - high[v, at]

    places = lax.broadcasted_iota(i32, (L, SLOTS), 0)
    parts = lax.broadcasted_iota(i32, (T, SLOTS), 0)
    none = jnp.zeros((L, SLOTS), bf16)

    def masked(values, s, part):
        return jnp.concatenate([jnp.where(part, values[v, s : s + 1, :], 0.0) for v in range(V + 1)], axis=0)

    def scatter(s):
        hits, values = [], []
        for i in range(2):
            target = place[s + i : s + i + 1, :]
            hits.append((places == (target & (L - 1))).astype(f32).astype(bf16))
            part = parts == ((target >> 8) + ((target >> 7) & 1) * R)
            values.append(jnp.concatenate([masked(x, s + i, part) for x in (high, low)], axis=0).astype(bf16))
        values = jnp.concatenate(values, axis=1)
        hits = [jnp.concatenate([hits[0], none], axis=1), jnp.concatenate([none, hits[1]], axis=1)]
        spread = lax.dot_general(
            values, jnp.concatenate(hits, axis=0), (((1,), (1,)), ((), ())), preferred_element_type=f32
        )
        spread = spread[:C] + spread[C:]
        keep = 1.0 - spread[Q:]
        for i in range(2):
            cols = slice(i * L, (i + 1) * L)
            for v in range(V):
                at = slice((s + i) * C + v * T, (s + i) * C + (v + 1) * T)
                prep[at, :] = spread[v * T : (v + 1) * T, cols] + keep[:, cols] * recv[at, :]

    def fluxes(g):
        for r in range(R):
            for h in range(2):
                u = [prep[pl.ds(g * N * C + v * T + h * R + r, N, stride=C), :] for v in range(V)]
                cols = slice(h * L, (h + 1) * L)
                inverse = 1.0 / u[0]
                va, vb = u[1] * inverse, u[2] * inverse
                pressure = 0.4 * (u[4] - 0.5 * (u[1] * u[1] + u[2] * u[2] + u[3] * u[3]) * inverse)
                total = u[4] + pressure
                flux_a = [u[1], u[1] * va + pressure, u[2] * va, u[3] * va, total * va]
                flux_b = [u[2], u[1] * vb, u[2] * vb + pressure, u[3] * vb, total * vb]
                for v in range(V):
                    at = slice((g * V + v) * B + r * N, (g * V + v) * B + (r + 1) * N)
                    field[at, cols] = u[v]
                    ah[at, cols], al[at, cols] = split(flux_a[v])
                    bh[at, cols], bl[at, cols] = split(flux_b[v])

    def products(g):
        own = jnp.bitwise_xor(half[0], g)
        (da_h, da_l), (db_h, db_l), (fa_h, fa_l), (fb_h, fb_l) = [split(here[own, m]) for m in range(4)]

        def section(v, at):
            slope = dot(da_h, ah[at]) + dot(da_h, al[at]) + dot(da_l, ah[at])
            slope += dot(bh[at], db_h) + dot(bl[at], db_h) + dot(bh[at], db_l)
            ah[at], al[at] = split(field[at] - section_weight * slope)

        def second(v, at):
            smooth = dot(ah[at], fb_h) + dot(al[at], fb_h) + dot(ah[at], fb_l)
            bh[at], bl[at] = split(smooth)

        def first(v, at):
            smooth = dot(fa_h, bh[at]) + dot(fa_h, bl[at]) + dot(fa_l, bh[at])
            for r in range(R):
                for h in range(2):
                    out[pl.ds(g * N * Q + v * T + h * R + r, N, stride=Q), :] = smooth[
                        r * N : (r + 1) * N, h * L : (h + 1) * L
                    ]

        return [
            (lambda stage=stage, v=v: stage(v, slice((g * V + v) * B, (g * V + v + 1) * B)))
            for stage in (section, second, first)
            for v in range(V)
        ]

    def arrived(g):
        own = jnp.bitwise_xor(half[0], g)
        pltpu.make_async_copy(mine, here.at[own], sems.at[own]).wait()

    pairs = list(range(0, 2 * N, 2))
    later = pairs[LEAD:]
    for s in pairs[:LEAD]:
        scatter(s)
    arrived(0)
    fluxes(0)
    for step in products(0):
        for s in later[:AHEAD]:
            scatter(s)
        later = later[AHEAD:]
        step()
    for s in later:
        scatter(s)
    fluxes(1)
    arrived(1)
    for step in products(1):
        step()


def unpack_kernel(lines, result, out, sems):
    copies = []
    for v in range(V):
        for r in range(R):
            for h in range(2):
                out[v, r, h * L : (h + 1) * L, :] = lines[pl.ds(v * T + h * R + r, L, stride=Q), :].T
        copies.append(pltpu.make_async_copy(out.at[v], result.at[v], sems.at[v]))
        copies[-1].start()
    for copy in copies:
        copy.wait()


def pack(donors, targets, flags, state, jacobian):
    return pl.pallas_call(
        pack_kernel,
        out_shape=jax.ShapeDtypeStruct((L, C, L), f32),
        in_specs=[HBM] * 6,
        out_specs=HBM,
        scratch_shapes=[
            pltpu.SMEM((2, N), i32),
            pltpu.SMEM((2, N), i32),
            pltpu.SMEM((R * B,), i32),
            pltpu.VMEM((T, L), i32),
            pltpu.VMEM((V * R * B, L), f32),
            pltpu.VMEM((R * B, L), f32),
            pltpu.VMEM(((V + 2) * SLOTS, L), f32),
            pltpu.VMEM((L * C, L), f32),
            pltpu.SemaphoreType.DMA((2 * V + 6,)),
        ],
        compiler_params=params(58),
        cost_estimate=cost(8_000_000),
        name="pack",
    )(
        donors.T,
        targets.T,
        flags.reshape(R * B),
        flags.reshape(T, L),
        state.reshape(V * R * B, L),
        jacobian.reshape(R * B, L),
    )


def matrices(*given):
    return pl.pallas_call(
        matrix_kernel,
        out_shape=jax.ShapeDtypeStruct((4, B, B), f32),
        in_specs=[VMEM] * 4,
        out_specs=VMEM,
        scratch_shapes=[pltpu.VMEM((2, B, L), f32)],
        compiler_params=params(8),
        cost_estimate=cost(2_000_000),
        name="matrices",
    )(*given)


def planes(half, recv, mine, theirs):
    return pl.pallas_call(
        plane_kernel,
        out_shape=jax.ShapeDtypeStruct((L * Q, L), f32),
        in_specs=[SMEM, VMEM, HBM, HBM],
        out_specs=VMEM,
        scratch_shapes=[
            pltpu.VMEM((L * C, L), f32),
            pltpu.VMEM((V + 1, L, SLOTS), f32),
            pltpu.VMEM((V + 1, L, SLOTS), f32),
            pltpu.VMEM((L, SLOTS), i32),
            pltpu.VMEM((2 * V * B, B), f32),
        ]
        + [pltpu.VMEM((2 * V * B, B), bf16)] * 4
        + [pltpu.VMEM((2, 4, B, B), f32), pltpu.SemaphoreType.DMA((2,))],
        compiler_params=params(40),
        cost_estimate=cost(8_000_000, 8_000_000_000),
        name="planes",
    )(half, recv, mine, theirs)


def unpack(lines):
    return pl.pallas_call(
        unpack_kernel,
        out_shape=jax.ShapeDtypeStruct((V, R, B, L), f32),
        in_specs=[VMEM],
        out_specs=HBM,
        scratch_shapes=[pltpu.VMEM((V, R, B, L), f32), pltpu.SemaphoreType.DMA((V,))],
        compiler_params=params(24),
        cost_estimate=cost(6_000_000),
        name="unpack",
    )(lines)


def exchange(value):
    return lax.all_to_all(value, ("half", "slab"), split_axis=0, concat_axis=0, tiled=True)


def local(state, jacobian, iblank, donor_blocks, recv_blocks, deriv_a, deriv_b, filter_a, filter_b):
    packed = pack(donor_blocks[0], recv_blocks[0], iblank[0], state[0], jacobian[0])
    recv = exchange(packed).reshape(L * C, L)
    mine = matrices(deriv_a[0], deriv_b[0], filter_a[0], filter_b[0])
    theirs = lax.ppermute(mine, "half", [(0, 1), (1, 0)])
    half = lax.axis_index("half").astype(i32)[None]
    lines = planes(half, recv, mine, theirs)
    result = exchange(lines.reshape(L, Q, L)).reshape(L * Q, L)
    return unpack(result)[None]


def solution(mesh):
    pairs = Mesh(mesh.devices.reshape(-1, 2, N), ("pair", "half", "slab"))
    grid = ("pair", "half")
    placed = (
        P(grid, None, "slab", None, None),
        P(grid, "slab", None, None),
        P(grid, "slab", None, None),
        P(grid, "slab", None),
        P(grid, "slab", None),
        P(grid, None, None),
        P(grid, None, None),
        P(grid, None, None),
        P(grid, None, None),
    )
    return jax.shard_map(
        local,
        mesh=pairs,
        in_specs=placed,
        out_specs=P(grid, None, "slab", None, None),
        check_vma=False,
    )
```

```python
import jax
import jax.numpy as jnp
from jax import lax
from jax.experimental import pallas as pl
from jax.experimental.pallas import tpu as pltpu
from jax.sharding import Mesh
from jax.sharding import PartitionSpec as P

V = 5
R = 4
N = 64
B = 256
L = 128
T = 2 * R
C = (V + 1) * T
Q = V * T
SLOTS = 128
LEAD = N
NOWHERE = 4 * R * B
EXTRA = Q
FREE = (1.0, 0.5, 0.0, 0.0, 2.5)

section_weight = 0.3
f32, bf16, i32 = jnp.float32, jnp.bfloat16, jnp.int32
VMEM = pl.BlockSpec(memory_space=pltpu.VMEM)
SMEM = pl.BlockSpec(memory_space=pltpu.SMEM)
HBM = pl.BlockSpec(memory_space=pltpu.HBM)


def params(mib):
    return pltpu.CompilerParams(vmem_limit_bytes=mib * 2**20)


def cost(nbytes, flops=0):
    return pl.CostEstimate(flops=flops, bytes_accessed=nbytes, transcendentals=0)


def pack_kernel(donors, targets, flags, holes, state, jacobian, sent, donor, target, flag, hole, u, jac, rows, out, sems):
    pairs = [(donors, donor), (targets, target), (flags, flag), (holes, hole), (jacobian, jac)]
    pairs += [(state.at[pl.ds(v * R * B, R * B)], u.at[pl.ds(v * R * B, R * B)]) for v in range(V)]
    fetch = [pltpu.make_async_copy(a, b, sems.at[i]) for i, (a, b) in enumerate(pairs)]
    for copy in [fetch[3]] + fetch[5:] + [fetch[4]] + fetch[:3]:
        copy.start()
    fetch[3].wait()
    lines_out = out.reshape(L, C, L)

    def send(v):
        at = pl.ds(v * T, T)
        copy = pltpu.make_async_copy(lines_out.at[:, at, :], sent.at[:, at, :], sems.at[V + 5 + v])
        copy.start()
        return copy

    sends = []
    for v in range(V):
        fetch[5 + v].wait()
        for r in range(R):
            for h in range(2):
                turned = u[(v * R + r) * B + h * L : (v * R + r) * B + (h + 1) * L, :].T
                out[pl.ds(v * T + h * R + r, L, stride=C), :] = jnp.where(
                    hole[2 * r + h : 2 * r + h + 1, :] == 0, FREE[v], turned
                )
        sends.append(send(v))
    for i in (0, 1, 2, 4):
        fetch[i].wait()
    lanes = lax.broadcasted_iota(i32, (1, SLOTS), 1)

    def body(s, row):
        for kk in range(2):
            k = kk * N + s
            t = donor[kk, s]
            rows[pl.ds(k, V, stride=SLOTS), :] = u[pl.ds(t, V, stride=R * B), :]
            rows[pl.ds(V * SLOTS + k, 1), :] = jac[pl.ds(t, 1), :]
            t = target[kk, s]
            rows[pl.ds((V + 1) * SLOTS + k, 1), :] = jac[pl.ds(t, 1), :]
            row = jnp.where(lanes == k, jnp.where(flag[t] == 2, t, NOWHERE), row)
        return row

    row = lax.fori_loop(0, N, body, jnp.full((1, SLOTS), NOWHERE, i32), unroll=8)
    for e in range(V + 2):
        out[pl.ds(EXTRA + e, L, stride=C), :] = rows[e * SLOTS : (e + 1) * SLOTS, :].T
    out[pl.ds(EXTRA + V + 2, L, stride=C), :] = jnp.broadcast_to(row.astype(f32), (L, SLOTS))
    sends.append(send(V))
    for copy in sends:
        copy.wait()


def matrix_kernel(da, db, fa, fb, out, rows):
    for at, matrix in ((0, da), (2, fa)):
        turned = matrix[...]
        for _ in range(2):
            for h in range(2):
                rows[h] = turned[:, h * L : (h + 1) * L]
            sorted_rows = [
                jnp.concatenate([rows[h, pl.ds(r, N, stride=R), :] for h in range(2)], axis=1) for r in range(R)
            ]
            turned = jnp.concatenate(sorted_rows, axis=0).T
        out[at] = turned
    out[1] = db[...].T
    out[3] = fb[...].T


def split(value):
    high = value.astype(bf16)
    return high, (value - high.astype(f32)).astype(bf16)


def dot(a, b):
    return jnp.dot(a, b, preferred_element_type=f32)


def plane_kernel(half, recv, mine, theirs, out, prep, high, low, place, field, ah, al, bh, bl, here, sems):
    fetch = [pltpu.make_async_copy(mine, here.at[0], sems.at[0]), pltpu.make_async_copy(theirs, here.at[1], sems.at[1])]
    for copy in fetch:
        copy.start()

    for g in range(2):
        def rows(grid, e):
            return recv[pl.ds(grid * N * C + EXTRA + e, N, stride=C), :]

        def swapped(e):
            turned = rows(1 - g, e).T
            return jnp.concatenate([turned[:N], turned[N:]], axis=1)

        at = slice(g * N, (g + 1) * N)
        weight = swapped(V)
        weight = weight / (weight + rows(g, V + 1))
        place[at] = rows(g, V + 2).astype(i32)
        for v in range(V + 1):
            value = weight if v == V else weight * swapped(v)
            high[v, at] = value.astype(bf16).astype(f32)
            low[v, at] = value - high[v, at]

    places = lax.broadcasted_iota(i32, (L, SLOTS), 0)
    parts = lax.broadcasted_iota(i32, (T, SLOTS), 0)
    none = jnp.zeros((L, SLOTS), bf16)

    def masked(values, s, part):
        return jnp.concatenate([jnp.where(part, values[v, s : s + 1, :], 0.0) for v in range(V + 1)], axis=0)

    def scatter(s):
        hits, values = [], []
        for i in range(2):
            target = place[s + i : s + i + 1, :]
            hits.append((places == (target & (L - 1))).astype(f32).astype(bf16))
            part = parts == ((target >> 8) + ((target >> 7) & 1) * R)
            values.append(jnp.concatenate([masked(x, s + i, part) for x in (high, low)], axis=0).astype(bf16))
        values = jnp.concatenate(values, axis=1)
        hits = [jnp.concatenate([hits[0], none], axis=1), jnp.concatenate([none, hits[1]], axis=1)]
        spread = lax.dot_general(
            values, jnp.concatenate(hits, axis=0), (((1,), (1,)), ((), ())), preferred_element_type=f32
        )
        spread = spread[:C] + spread[C:]
        keep = 1.0 - spread[Q:]
        for i in range(2):
            cols = slice(i * L, (i + 1) * L)
            for v in range(V):
                at = slice((s + i) * C + v * T, (s + i) * C + (v + 1) * T)
                prep[at, :] = spread[v * T : (v + 1) * T, cols] + keep[:, cols] * recv[at, :]

    def fluxes(g):
        for r in range(R):
            for h in range(2):
                u = [prep[pl.ds(g * N * C + v * T + h * R + r, N, stride=C), :] for v in range(V)]
                cols = slice(h * L, (h + 1) * L)
                inverse = 1.0 / u[0]
                va, vb = u[1] * inverse, u[2] * inverse
                pressure = 0.4 * (u[4] - 0.5 * (u[1] * u[1] + u[2] * u[2] + u[3] * u[3]) * inverse)
                total = u[4] + pressure
                flux_a = [u[1], u[1] * va + pressure, u[2] * va, u[3] * va, total * va]
                flux_b = [u[2], u[1] * vb, u[2] * vb + pressure, u[3] * vb, total * vb]
                for v in range(V):
                    at = slice((g * V + v) * B + r * N, (g * V + v) * B + (r + 1) * N)
                    field[at, cols] = u[v]
                    ah[at, cols], al[at, cols] = split(flux_a[v])
                    bh[at, cols], bl[at, cols] = split(flux_b[v])

    def products(g):
        own = jnp.bitwise_xor(half[0], g)
        (da_h, da_l), (db_h, db_l), (fa_h, fa_l), (fb_h, fb_l) = [split(here[own, m]) for m in range(4)]

        def section(v, at):
            slope = dot(da_h, ah[at]) + dot(da_h, al[at]) + dot(da_l, ah[at])
            slope += dot(bh[at], db_h) + dot(bl[at], db_h) + dot(bh[at], db_l)
            ah[at], al[at] = split(field[at] - section_weight * slope)

        def second(v, at):
            smooth = dot(ah[at], fb_h) + dot(al[at], fb_h) + dot(ah[at], fb_l)
            bh[at], bl[at] = split(smooth)

        def first(v, at):
            smooth = dot(fa_h, bh[at]) + dot(fa_h, bl[at]) + dot(fa_l, bh[at])
            for r in range(R):
                for h in range(2):
                    out[pl.ds(g * N * Q + v * T + h * R + r, N, stride=Q), :] = smooth[
                        r * N : (r + 1) * N, h * L : (h + 1) * L
                    ]

        return [
            (lambda stage=stage, v=v: stage(v, slice((g * V + v) * B, (g * V + v + 1) * B)))
            for stage in (section, second, first)
            for v in range(V)
        ]

    pairs = list(range(0, 2 * N, 2))
    later = pairs[LEAD:]
    for s in pairs[:LEAD]:
        scatter(s)
    for copy in fetch:
        copy.wait()
    fluxes(0)
    for step in products(0):
        for s in later[:1]:
            scatter(s)
        later = later[1:]
        step()
    for s in later:
        scatter(s)
    fluxes(1)
    for step in products(1):
        step()


def unpack_kernel(lines, result, out, sems):
    copies = []
    for v in range(V):
        for r in range(R):
            for h in range(2):
                out[v, r, h * L : (h + 1) * L, :] = lines[pl.ds(v * T + h * R + r, L, stride=Q), :].T
        copies.append(pltpu.make_async_copy(out.at[v], result.at[v], sems.at[v]))
        copies[-1].start()
    for copy in copies:
        copy.wait()


def pack(donors, targets, flags, state, jacobian):
    return pl.pallas_call(
        pack_kernel,
        out_shape=jax.ShapeDtypeStruct((L, C, L), f32),
        in_specs=[HBM] * 6,
        out_specs=HBM,
        scratch_shapes=[
            pltpu.SMEM((2, N), i32),
            pltpu.SMEM((2, N), i32),
            pltpu.SMEM((R * B,), i32),
            pltpu.VMEM((T, L), i32),
            pltpu.VMEM((V * R * B, L), f32),
            pltpu.VMEM((R * B, L), f32),
            pltpu.VMEM(((V + 2) * SLOTS, L), f32),
            pltpu.VMEM((L * C, L), f32),
            pltpu.SemaphoreType.DMA((2 * V + 6,)),
        ],
        compiler_params=params(58),
        cost_estimate=cost(8_000_000),
        name="pack",
    )(
        donors.T,
        targets.T,
        flags.reshape(R * B),
        flags.reshape(T, L),
        state.reshape(V * R * B, L),
        jacobian.reshape(R * B, L),
    )


def matrices(*given):
    return pl.pallas_call(
        matrix_kernel,
        out_shape=jax.ShapeDtypeStruct((4, B, B), f32),
        in_specs=[VMEM] * 4,
        out_specs=VMEM,
        scratch_shapes=[pltpu.VMEM((2, B, L), f32)],
        compiler_params=params(8),
        cost_estimate=cost(2_000_000),
        name="matrices",
    )(*given)


def planes(half, recv, mine, theirs):
    return pl.pallas_call(
        plane_kernel,
        out_shape=jax.ShapeDtypeStruct((L * Q, L), f32),
        in_specs=[SMEM, VMEM, HBM, HBM],
        out_specs=VMEM,
        scratch_shapes=[
            pltpu.VMEM((L * C, L), f32),
            pltpu.VMEM((V + 1, L, SLOTS), f32),
            pltpu.VMEM((V + 1, L, SLOTS), f32),
            pltpu.VMEM((L, SLOTS), i32),
            pltpu.VMEM((2 * V * B, B), f32),
        ]
        + [pltpu.VMEM((2 * V * B, B), bf16)] * 4
        + [pltpu.VMEM((2, 4, B, B), f32), pltpu.SemaphoreType.DMA((2,))],
        compiler_params=params(40),
        cost_estimate=cost(8_000_000, 8_000_000_000),
        name="planes",
    )(half, recv, mine, theirs)


def unpack(lines):
    return pl.pallas_call(
        unpack_kernel,
        out_shape=jax.ShapeDtypeStruct((V, R, B, L), f32),
        in_specs=[VMEM],
        out_specs=HBM,
        scratch_shapes=[pltpu.VMEM((V, R, B, L), f32), pltpu.SemaphoreType.DMA((V,))],
        compiler_params=params(24),
        cost_estimate=cost(6_000_000),
        name="unpack",
    )(lines)


def exchange(value):
    return lax.all_to_all(value, ("half", "slab"), split_axis=0, concat_axis=0, tiled=True)


def local(state, jacobian, iblank, donor_blocks, recv_blocks, deriv_a, deriv_b, filter_a, filter_b):
    packed = pack(donor_blocks[0], recv_blocks[0], iblank[0], state[0], jacobian[0])
    recv = exchange(packed).reshape(L * C, L)
    mine = matrices(deriv_a[0], deriv_b[0], filter_a[0], filter_b[0])
    theirs = lax.ppermute(mine, "half", [(0, 1), (1, 0)])
    half = lax.axis_index("half").astype(i32)[None]
    lines = planes(half, recv, mine, theirs)
    result = exchange(lines.reshape(L, Q, L)).reshape(L * Q, L)
    return unpack(result)[None]


def solution(mesh):
    pairs = Mesh(mesh.devices.reshape(-1, 2, N), ("pair", "half", "slab"))
    grid = ("pair", "half")
    placed = (
        P(grid, None, "slab", None, None),
        P(grid, "slab", None, None),
        P(grid, "slab", None, None),
        P(grid, "slab", None),
        P(grid, "slab", None),
        P(grid, None, None),
        P(grid, None, None),
        P(grid, None, None),
        P(grid, None, None),
    )
    return jax.shard_map(
        local,
        mesh=pairs,
        in_specs=placed,
        out_specs=P(grid, None, "slab", None, None),
        check_vma=False,
    )
```
